32 devices in a mesh: section: 4 (over z), row: 2 (over core), col: 4 (over y, x).
Axes of the slice: x: 2, y: 2, z: 4, core: 2. Of those that a mesh axis runs over, the one named last changes fastest.
Arguments:
- arriving: bfloat16 [4, 8, 16384], P('section', ('row', 'col')), may hold values from -64 to 64
- entering: bfloat16 [3, 8, 16384], P(None, ('row', 'col')), may hold values from -64 to 64
- gain: bfloat16 [4, 16384], P('section'), may hold values from 0.099609375 to 1.8984375
- kv_weight: bfloat16 [4, 16384, 1024], P('section', 'row', 'col'), may hold values from -0.046875 to 0.046875
- queries: bfloat16 [4, 4, 8, 8192], P('section', None, ('row', 'col')), may hold values from -150 to 150
- cache_keys: bfloat16 [4, 4, 8, 128, 512], P('section', None, ('row', 'col')), may hold values from -6 to 6
- cache_values: bfloat16 [4, 4, 8, 128, 512], P('section', None, ('row', 'col')), may hold values from -6 to 6
- lengths: int32 [7, 8], P(None, ('row', 'col')), may hold values from 2 to 128, as said below
Outputs:
- layer_out: bfloat16 [4, 4, 8, 16384], P('section', None, ('row', 'col'))
The draws below stay inside these ranges and needn't reach their ends.
Inputs may be any that keep to these rules, and one draw needn't show every extreme that they name: Every row of lengths has a request with exactly 128 cached tokens, at a position drawn from the seed.
All inputs are finite; a program needn't handle non-finite values.
Results may differ from the reference program's by a relative error of at most 0.0034.
Values may be sent and summed in bfloat16 or wider, within the bound.
A program may use at most 64 MiB of HBM per device.

```python
import math
import jax
import jax.numpy as jnp
import numpy as np
from jax import lax

D = 16384
QH = 64
KVH = 4
HD = 128
LMAX = 128
TICKS = 4
KVW = 1024
LAYERS = 4
MB = 8
ENTRIES = 7


def shared_keys(key):
    base = jnp.clip(jax.random.normal(jax.random.fold_in(key, 101), (LAYERS, TICKS, MB, LMAX, KVH * HD), jnp.float32), -6.0, 6.0)
    return base


def draw_cache_keys(key, part):
    base = shared_keys(key)
    return base.astype(jnp.bfloat16)


def draw_queries(key, part):
    drawn = jnp.clip(jax.random.normal(jax.random.fold_in(key, 103), (LAYERS, TICKS, MB, QH * HD), jnp.float32), -6.0, 6.0)
    return drawn.astype(jnp.bfloat16)


def scaled_rows(key, salt, count):
    drawn = jnp.clip(jax.random.normal(jax.random.fold_in(key, salt), (count, MB, D), jnp.float32), -4.0, 4.0)
    low = math.log(0.4)
    high = math.log(4.0)
    row_scale = jnp.exp(jax.random.uniform(jax.random.fold_in(key, salt + 1), (count, MB, 1), jnp.float32, low, high))
    col_scale = jnp.exp(jax.random.uniform(jax.random.fold_in(key, salt + 2), (count, 1, D), jnp.float32, low, high))
    return (drawn * row_scale * col_scale).astype(jnp.bfloat16)


def draw_arriving(key, part):
    return scaled_rows(key, 201, LAYERS)


def draw_entering(key, part):
    return scaled_rows(key, 301, TICKS - 1)


def draw_lengths(key, part):
    first = jax.random.randint(jax.random.fold_in(key, 401), (ENTRIES, MB), 2, LMAX + 1)
    second = jax.random.randint(jax.random.fold_in(key, 402), (ENTRIES, MB), 2, LMAX + 1)
    longest = jax.random.randint(jax.random.fold_in(key, 403), (ENTRIES, 1), 0, MB)
    base = jnp.minimum(first, second)
    return jnp.where(jnp.arange(MB)[None, :] == longest, LMAX, base).astype(jnp.int32)


def steps_of(own_key, extent, cuts, least, top_value):
    factor_of, own = 1.0, jax.random.fold_in(own_key, 6)
    for axis_at, shards_of in cuts:
        steps = jnp.exp(jax.random.uniform(jax.random.fold_in(own, axis_at), (shards_of,), jnp.float32, least / len(cuts), top_value / len(cuts)))
        factor_of = factor_of * jnp.repeat(steps, extent[axis_at] // shards_of).reshape([-1 if axis == axis_at else 1 for axis in range(len(extent))])
    return factor_of


def gaussian(own_key, extent, scale, reach, split=(), held_as=jnp.bfloat16):
    drawn = jax.random.normal(own_key, extent, jnp.float32) * scale
    if len(split) > 0:
        drawn = steps_of(own_key, extent, split, -0.22, 0.18) * drawn
    return jnp.clip(drawn, min=-reach, max=reach).astype(held_as)


def setup_inputs(seed: int = 0) -> dict:
    key_of = jax.random.split(jax.random.key(seed), 9)
    return {
        "arriving": draw_arriving(jax.random.fold_in(key_of[8], 71), 0),
        "entering": draw_entering(jax.random.fold_in(key_of[8], 71), 0),
        "gain": jnp.clip(1.0 + 0.18 * jax.random.normal(key_of[2], (LAYERS, D), jnp.float32), 0.099609375, 1.8984375).astype(jnp.bfloat16),
        "kv_weight": gaussian(key_of[3], (LAYERS, D, KVW), D ** -0.5, 0.046875, ((0, 4), (1, 2), (2, 4))),
        "queries": draw_queries(jax.random.fold_in(key_of[8], 71), 0),
        "cache_keys": draw_cache_keys(jax.random.fold_in(key_of[8], 71), 0),
        "cache_values": gaussian(key_of[6], (LAYERS, TICKS, MB, LMAX, KVH * HD), 1.0, 6.0, ((0, 4), (2, 8))),
        "lengths": draw_lengths(jax.random.fold_in(key_of[8], 71), 0),
    }


def rotate(keys, positions):
    half = HD // 2
    steps_up = jnp.arange(half).astype(jnp.float32)
    inverse = jnp.exp(-jnp.log(jnp.float32(500000.0)) * steps_up / half)
    angle = positions.astype(jnp.float32)[:, None] * inverse[None, :]
    cosine = jnp.cos(angle)[:, None, :]
    sine = jnp.sin(angle)[:, None, :]
    first = keys[..., :half]
    second = keys[..., half:]
    return jnp.concatenate([first * cosine - second * sine, second * cosine + first * sine], axis=-1)

def layer(rows, gain_row, weight, queries, keys, values, lengths):
    count = rows.shape[0]
    wide = rows.astype(jnp.float32)
    scale = lax.rsqrt(lax.optimization_barrier(jnp.mean(wide * wide, axis=1, keepdims=True)) + 1e-05)
    normed = (wide * scale * gain_row.astype(jnp.float32)[None, :]).astype(jnp.bfloat16)
    fresh = jnp.dot(normed, weight, preferred_element_type=jnp.float32).reshape(count, KVH, 2, HD)
    new_key = rotate(fresh[:, :, 0, :], lengths).astype(jnp.bfloat16)
    new_value = fresh[:, :, 1, :].astype(jnp.bfloat16)
    factor = 1.0 / np.sqrt(HD)
    grouped = queries.reshape(count, KVH, QH // KVH, HD).astype(jnp.float32)
    cached = keys.reshape(count, LMAX, KVH, HD).astype(jnp.float32)
    stored = values.reshape(count, LMAX, KVH, HD).astype(jnp.float32)
    scores = jnp.einsum('rghd,rlgd->rghl', grouped, cached) * factor
    live = jnp.arange(LMAX)[None, :] < lengths[:, None]
    scores = jnp.where(live[:, None, None, :], scores, jnp.float32(-1e+30))
    own = jnp.einsum('rghd,rgd->rgh', grouped, new_key.astype(jnp.float32)) * factor
    top = jnp.maximum(lax.optimization_barrier(jnp.max(scores, axis=-1)), own)
    weights = jnp.exp(scores - top[..., None])
    own_weight = jnp.exp(own - top)
    total = lax.optimization_barrier(jnp.sum(weights, axis=-1)) + own_weight
    probs = (weights / total[..., None]).astype(jnp.bfloat16)
    own_prob = (own_weight / total).astype(jnp.bfloat16)
    mixed = jnp.einsum('rghl,rlgd->rghd', probs.astype(jnp.float32), stored)
    mixed = mixed + own_prob.astype(jnp.float32)[..., None] * new_value.astype(jnp.float32)[:, :, None, :]
    heads_width = QH * HD
    mixed = mixed.reshape(count, heads_width)
    joined = jnp.concatenate([wide[:, :heads_width] + mixed, wide[:, heads_width:]], axis=1)
    return joined.astype(jnp.bfloat16)

def reference(arriving, entering, gain, kv_weight, queries, cache_keys, cache_values, lengths):
    rows_now = arriving
    previous = arriving
    results = []
    for tick in range(TICKS):
        if tick > 0:
            rows_now = jnp.concatenate([entering[tick - 1][None], previous[:-1]], axis=0)
        picked = lengths[tick + LAYERS - 1 - np.arange(LAYERS)]
        previous = lax.map(lambda item: layer(*item), (rows_now, gain, kv_weight, queries[:, tick], cache_keys[:, tick], cache_values[:, tick], picked))
        results.append(previous)
    return jnp.stack(results, axis=1)
```

```python
import functools

import jax
import jax.numpy as jnp
import numpy as np
from jax import lax
from jax.experimental import pallas as pl
from jax.experimental.pallas import tpu as pltpu
from jax.sharding import PartitionSpec as P

QH = 64
KVH = 4
HD = 128
GROUP = QH // KVH
MESH = pl.DeviceIdType.MESH


def shifted(array, axis, by):
    devices = lax.axis_size(axis)
    pairs = [(i, i + by) for i in range(devices) if 0 <= i + by < devices]
    return lax.ppermute(array, axis, pairs)


def rotate(keys, positions):
    half = HD // 2
    steps_up = jnp.arange(half).astype(jnp.float32)
    inverse = jnp.exp(-jnp.log(jnp.float32(500000.0)) * steps_up / half)
    angle = positions.astype(jnp.float32)[:, None] * inverse[None, :]
    cosine = jnp.cos(angle)[:, None, :]
    sine = jnp.sin(angle)[:, None, :]
    first = keys[..., :half]
    second = keys[..., half:]
    return jnp.concatenate(
        [first * cosine - second * sine, second * cosine + first * sine], axis=-1
    )


def attend(query_row, keys, values, new_key, new_value, length):
    slots = keys.shape[0]
    factor = 1.0 / np.sqrt(HD)
    grouped = query_row.reshape(KVH, QH // KVH, HD)
    cached = keys.reshape(slots, KVH, HD)
    stored = values.reshape(slots, KVH, HD)
    scores = (
        jnp.einsum("ghd,lgd->ghl", grouped, cached, preferred_element_type=jnp.float32) * factor
    )
    live = jnp.arange(slots) < length
    scores = jnp.where(live[None, None, :], scores, jnp.float32(-1e30))
    own = jnp.einsum("ghd,gd->gh", grouped, new_key, preferred_element_type=jnp.float32) * factor
    top = jnp.maximum(jnp.max(scores, axis=-1), own)
    weights = jnp.exp(scores - top[..., None])
    own_weight = jnp.exp(own - top)
    total = jnp.sum(weights, axis=-1) + own_weight
    probs = (weights / total[..., None]).astype(jnp.bfloat16)
    own_prob = (own_weight / total).astype(jnp.bfloat16)
    mixed = jnp.einsum("ghl,lgd->ghd", probs, stored, preferred_element_type=jnp.float32)
    mixed = (
        mixed + own_prob.astype(jnp.float32)[..., None] * new_value.astype(jnp.float32)[:, None, :]
    )
    return mixed.reshape(1, QH * HD)


def per_device_general(arriving, entering, gain, kv_weight, queries, cache_keys, cache_values, lengths):
    section_at = lax.axis_index("section")
    row_at = lax.axis_index("row")
    rows_count = lax.axis_size("row")
    cols_count = lax.axis_size("col")
    ticks = queries.shape[1]
    layers_all = lengths.shape[0] - ticks + 1
    width = arriving.shape[2]
    half_width = width // rows_count
    heads_width = QH * HD
    weight = kv_weight[0]
    gain_row = gain[0].astype(jnp.float32)
    current = arriving[0]
    outputs = []
    for tick in range(ticks):
        if tick > 0:
            passed = shifted(current, "section", 1)
            current = jnp.where(section_at == 0, entering[tick - 1], passed)
        length = lax.dynamic_index_in_dim(
            lengths[:, 0], tick - section_at + layers_all - 1, 0, keepdims=False
        )
        wide = current.astype(jnp.float32)
        scale = lax.rsqrt(jnp.mean(wide * wide, axis=1, keepdims=True) + 1e-05)
        normed = (wide * scale * gain_row[None, :]).astype(jnp.bfloat16)
        mine = lax.dynamic_slice_in_dim(
            lax.all_gather(normed, ("row", "col"), axis=0, tiled=True),
            row_at * half_width,
            half_width,
            1,
        )
        gathered = jnp.dot(mine, weight, preferred_element_type=jnp.float32)
        partial_rows = jnp.swapaxes(gathered.reshape(rows_count, cols_count, -1), 0, 1)
        summed = lax.psum_scatter(partial_rows, "row", scatter_dimension=1, tiled=True)
        fresh = lax.all_to_all(summed, "col", split_axis=0, concat_axis=2, tiled=True)
        fresh = fresh.reshape(KVH, 2, HD)
        new_key = rotate(fresh[None, :, 0, :], length[None])[0].astype(jnp.bfloat16)
        new_value = fresh[:, 1, :].astype(jnp.bfloat16)
        mixed = attend(
            queries[0, tick, 0],
            cache_keys[0, tick, 0],
            cache_values[0, tick, 0],
            new_key,
            new_value,
            length,
        )
        joined = jnp.concatenate([wide[:, :heads_width] + mixed, wide[:, heads_width:]], axis=1)
        current = joined.astype(jnp.bfloat16)
        outputs.append(current)
    return jnp.stack(outputs, axis=0)[None]


def relay_kernel(
    sections, ticks, cols, requests,
    lens_ref, arr_ref, ent_ref, gain_ref, w_ref, q_ref, k_ref, v_ref, cs_ref,
    out_ref,
    wv, xj, xh, xs, qb_src, qb_buf, misc_src, misc_buf, p_src, p_buf, hj, lse_hj, xo, oj,
    w_sem, send_sem, xj_sem, xh_sem, qb_sem, misc_sem, p_sem, z_sem, out_sem,
):
    f32, bf16 = jnp.float32, jnp.bfloat16
    me_s, me_r, me_c = lax.axis_index("section"), lax.axis_index("row"), lax.axis_index("col")
    me_j = me_r * cols + me_c
    factor = 1.0 / np.sqrt(HD)
    width = 2.0 * QH * HD
    later = ticks - 1

    def at(s, r, c):
        return {"section": s, "row": r, "col": c}

    barrier = pltpu.get_barrier_semaphore()

    def greet(cond, where):
        def do():
            pl.semaphore_signal(barrier, inc=1, device_id=where, device_id_type=MESH)
        if cond is True:
            do()
        else:
            pl.when(cond)(do)

    for dr in range(2):
        for dc in range(cols):
            if dr or dc:
                greet(True, at(me_s, (me_r + dr) % 2, (me_c + dc) % cols))
    for d in range(1, ticks):
        greet(me_s >= d, at(me_s - d, me_r, me_c))
    for dc in range(1, cols):
        greet((me_r == 0) & (me_s >= 1), at(me_s - 1, me_r, (me_c + dc) % cols))

    depth = w_ref.shape[0] // cols
    def w_copy(b):
        return pltpu.make_async_copy(
            w_ref.at[pl.ds(b * depth, depth)], wv.at[pl.ds(b * depth, depth)], w_sem.at[b])
    for b in range(cols):
        w_copy(b).start()

    out_ref[0, QH:] = arr_ref[QH:]
    for t in range(1, ticks):
        @pl.when(me_s < t)
        def _():
            out_ref[t, QH:] = ent_ref[t - 1 - me_s, QH:]

    reach = jnp.minimum(ticks - 1, sections - 1 - me_s)
    onward = jnp.where((me_r == 0) & (me_s + 1 < sections), cols - 1, 0)
    pl.semaphore_wait(barrier, 2 * cols - 1 + reach + onward)

    sent = []
    on_chain, off_chain, has_next = me_r == 0, me_r == 1, me_s + 1 < sections
    chain_next = on_chain & has_next

    def remote(cond, src, dst, rsem, where, held=None, like=None):
        number = len(sent)
        sent.append((cond if held is None else held, (lambda: src) if like is None else like))

        def go():
            pltpu.make_async_remote_copy(
                src_ref=src, dst_ref=dst, send_sem=send_sem.at[number], recv_sem=rsem,
                device_id=where, device_id_type=MESH).start()
        if cond is True:
            go()
        else:
            pl.when(cond)(go)

    def local(cond, src, dst, rsem):
        def go():
            pltpu.make_async_copy(src, dst, rsem).start()
        pl.when(cond)(go)

    def push(cond, src_of, dst, rsem, row):
        for dc in range(cols):
            col = (me_c + dc) % cols
            if dc == 0:
                here = me_r == row if cond is True else cond & (me_r == row)
                away = me_r != row if cond is True else cond & (me_r != row)
                local(here, src_of(col), dst, rsem)
                remote(away, src_of(col), dst, rsem, at(me_s, row, col))
            else:
                remote(cond, src_of(col), dst, rsem, at(me_s, row, col))

    def landed(ref, sem):
        pltpu.make_async_copy(ref, ref, sem).wait()

    def cache_part(t):
        length = lens_ref[t]
        lane = lax.broadcasted_iota(jnp.int32, (GROUP, HD), 1)
        sub = lax.broadcasted_iota(jnp.int32, (GROUP, HD), 0)
        lse_row = jnp.zeros((1, HD), f32)
        for g in range(KVH):
            qg = q_ref[t, g * GROUP:(g + 1) * GROUP, :]
            kg = k_ref[t, :, g * HD:(g + 1) * HD]
            vg = v_ref[t, :, g * HD:(g + 1) * HD]
            s = lax.dot_general(qg, kg, (((1,), (1,)), ((), ())), preferred_element_type=f32) * factor
            s = jnp.where(lane < length, s, f32(-1e30))
            top = jnp.max(s, axis=1, keepdims=True)
            e = jnp.exp(s - top)
            total = jnp.sum(e, axis=1, keepdims=True)
            base = jnp.dot((e / total).astype(bf16), vg, preferred_element_type=f32)
            qb_src[g, t, :GROUP, :] = qg
            qb_src[g, t, GROUP:, :] = base.astype(bf16)
            lse = top + jnp.log(total)
            lse_row += jnp.sum(jnp.where(lane == sub + g * GROUP, lse, 0.0), axis=0, keepdims=True)
        misc_src[t * 8:t * 8 + 8, :] = cs_ref[t]
        misc_src[t * 8 + 2:t * 8 + 3, :] = lse_row

    def push_cache_part(first, count, number):
        span = pl.ds(first, count)
        push(True, lambda col: qb_src.at[col, span], qb_buf.at[me_j, span], qb_sem.at[number], 0)
        push(True, lambda col: misc_src.at[pl.ds(first * 8, count * 8)],
             misc_buf.at[me_j, pl.ds(first * 8, count * 8)], misc_sem.at[number], 0)

    push(True, lambda col: arr_ref.at[pl.ds(0, QH)], xj.at[0, me_j], xj_sem.at[0], 0)
    push(True, lambda col: arr_ref.at[pl.ds(QH, QH)], xj.at[0, me_j], xj_sem.at[0], 1)
    for d in range(1, ticks):
        remote(me_s + d < sections, arr_ref.at[pl.ds(QH, QH)], out_ref.at[d, pl.ds(QH, QH)],
               z_sem.at[d], at(me_s + d, me_r, me_c))
    for t in range(1, ticks):
        push(me_s == 0, lambda col: ent_ref.at[t - 1, pl.ds(0, QH)], xj.at[t, me_j], xj_sem.at[t], 0)

    cache_part(0)
    push_cache_part(0, 1, 0)

    def rest():
        for t in range(1, ticks):
            @pl.when(me_s >= t)
            def _():
                landed(out_ref.at[t, pl.ds(QH, QH)], z_sem.at[t])
            push(True, lambda col: out_ref.at[t, pl.ds(QH, QH)], xj.at[t, me_j], xj_sem.at[t], 1)
        for t in range(1, ticks):
            cache_part(t)
        push_cache_part(1, later, 1)

    def turned(t):
        return jnp.swapaxes(xj[t].astype(f32), 0, 1)

    def lanes(x, gains, b):
        parts = [x[h] * gains[h:h + 1] for h in range(b * GROUP, (b + 1) * GROUP)]
        return jnp.concatenate(parts, axis=1)

    def squares(x):
        return jnp.sum(jnp.sum(x * x, axis=0), axis=1, keepdims=True)

    def static_part(first, count):
        gains = gain_ref[QH:].astype(f32)
        for t in range(first, first + count):
            landed(xj.at[t], xj_sem.at[t])
        xt = [turned(t) for t in range(first, first + count)]
        total = jnp.zeros((count * requests, 2 * HD), f32)
        for b in range(cols):
            lhs = jnp.concatenate([lanes(x, gains, b) for x in xt], axis=0).astype(bf16)
            total += jnp.dot(lhs, wv[b * depth:(b + 1) * depth, :], preferred_element_type=f32)
        for i in range(count):
            p_src[first + i, :, :2 * HD] = total[i * requests:(i + 1) * requests]
            p_src[first + i, :, 2 * HD:] = jnp.broadcast_to(squares(xt[i]), (requests, HD))

    def prepare(t):
        if t <= 1:
            number, first, count = (0, 0, 1) if t == 0 else (1, 1, later)
            landed(qb_buf.at[:, pl.ds(first, count)], qb_sem.at[number])
            landed(misc_buf.at[:, pl.ds(first * 8, count * 8)], misc_sem.at[number])
        hj[...] = jnp.swapaxes(qb_buf[:, t].astype(f32), 0, 1)
        rows = jnp.concatenate([misc_buf[j, t * 8 + 2:t * 8 + 3, :] for j in range(requests)], axis=0)
        lane = lax.broadcasted_iota(jnp.int32, (GROUP, requests, HD), 2)
        head = lax.broadcasted_iota(jnp.int32, (GROUP, requests, HD), 0) + me_c * GROUP
        picked = jnp.sum(jnp.where(lane == head, rows[None], 0.0), axis=2, keepdims=True)
        lse_hj[...] = jnp.broadcast_to(picked, (GROUP, requests, HD))

    def chain(t):
        gains = gain_ref[:QH].astype(f32)
        if t == 0:
            landed(xj.at[0], xj_sem.at[0])
            xs[...] = turned(0)
        else:
            @pl.when(me_s == 0)
            def _():
                landed(xj.at[t], xj_sem.at[t])
                xs[...] = turned(t)

            @pl.when(me_s > 0)
            def _():
                landed(xh.at[t - 1], xh_sem.at[t - 1])
                xs[...] = xh[t - 1].astype(f32).reshape(QH, requests, HD)
        x = xs[...]
        fresh = jnp.zeros((requests, 2 * HD), f32)
        for b in range(cols):
            fresh += jnp.dot(lanes(x, gains, b).astype(bf16), wv[b * depth:(b + 1) * depth, :],
                             preferred_element_type=f32)
        power = squares(x)
        if t <= 1:
            span = pl.ds(0, 1) if t == 0 else pl.ds(1, later)
            landed(p_buf.at[span], p_sem.at[t])
        power += p_buf[t, :, 2 * HD:2 * HD + 1]
        fresh = (fresh + p_buf[t, :, :2 * HD]) * lax.rsqrt(power / width + 1e-05)
        cosine = jnp.concatenate([misc_buf[j, t * 8:t * 8 + 1, :] for j in range(requests)], axis=0)
        sine = jnp.concatenate([misc_buf[j, t * 8 + 1:t * 8 + 2, :] for j in range(requests)], axis=0)
        key = fresh[:, :HD]
        key = key * cosine + pltpu.roll(key, HD // 2, 1) * sine
        key = key.astype(bf16).astype(f32)
        value = fresh[:, HD:].astype(bf16).astype(f32)
        q = hj[:GROUP]
        base = hj[GROUP:]
        lse = lse_hj[...]
        own = jnp.sum(q * key[None], axis=2, keepdims=True) * factor
        top = jnp.maximum(lse, own)
        old_weight = jnp.exp(lse - top)
        own_weight = jnp.exp(own - top)
        inverse = 1.0 / (old_weight + own_weight)
        own_prob = (own_weight * inverse).astype(bf16).astype(f32)
        mixed = base * (old_weight * inverse) + own_prob * value[None]
        mine = xs[pl.ds(pl.multiple_of(me_c * GROUP, GROUP), GROUP)] + mixed
        block = pl.ds(pl.multiple_of(me_c * GROUP, GROUP), GROUP)
        if t + 1 < ticks:
            rows = requests * GROUP
            xo[t] = mine.reshape(rows, HD).astype(bf16)
            for dc in range(cols):
                remote(has_next, xo.at[t],
                       xh.at[t, pl.ds(pl.multiple_of(me_c * rows, rows), rows)],
                       xh_sem.at[t], at(me_s + 1, 0, (me_c + dc) % cols), held=chain_next, like=lambda: xo.at[t])
        oj[t] = jnp.swapaxes(mine, 0, 1).astype(bf16)
        for r in range(2):
            for dc in range(cols):
                col = (me_c + dc) % cols
                src = oj.at[t, r * cols + col]
                dst = out_ref.at[t, block]
                if r == 0 and dc == 0:
                    pltpu.make_async_copy(src, dst, out_sem.at[t]).start()
                else:
                    remote(True, src, dst, out_sem.at[t], at(me_s, r, col),
                           held=on_chain, like=lambda: oj.at[t, 0])

    def push_static(first, count):
        span = pl.ds(first, count)
        remote(True, p_src.at[span], p_buf.at[span], p_sem.at[0 if first == 0 else 1],
               at(me_s, 0, me_c), held=off_chain, like=lambda: p_src.at[span])

    for b in range(cols):
        w_copy(b).wait()

    @pl.when(me_r == 0)
    def _():
        prepare(0)
        chain(0)

    @pl.when(me_r == 1)
    def _():
        static_part(0, 1)
        push_static(0, 1)

    rest()

    @pl.when(me_r == 1)
    def _():
        static_part(1, later)
        push_static(1, later)

    @pl.when(me_r == 0)
    def _():
        for t in range(1, ticks):
            prepare(t)
            chain(t)

    for t in range(ticks):
        landed(out_ref.at[t, pl.ds(0, QH)], out_sem.at[t])
    for number, (cond, like) in enumerate(sent):
        def done(number=number, like=like):
            landed(like(), send_sem.at[number])
        if cond is True:
            done()
        else:
            pl.when(cond)(done)


def per_device(arriving, entering, gain, kv_weight, queries, cache_keys, cache_values, lengths):
    sections, cols = lax.axis_size("section"), lax.axis_size("col")
    ticks = queries.shape[1]
    requests = 2 * cols
    layers_all = lengths.shape[0] - ticks + 1
    start = layers_all - 1 - lax.axis_index("section")
    lens = lax.dynamic_slice_in_dim(lengths[:, 0], start, ticks, 0)
    half = HD // 2
    inverse = jnp.exp(-jnp.log(jnp.float32(500000.0)) * jnp.arange(half).astype(jnp.float32) / half)
    angle = lens.astype(jnp.float32)[:, None] * inverse[None, :]
    cosine, sine = jnp.cos(angle), jnp.sin(angle)
    turn = jnp.stack([jnp.concatenate([cosine, cosine], 1), jnp.concatenate([-sine, sine], 1)], axis=1)
    turn = jnp.pad(turn, ((0, 0), (0, 6), (0, 0)))
    blocks = arriving.shape[2] // HD
    bf16, f32 = jnp.bfloat16, jnp.float32
    vmem = pl.BlockSpec(memory_space=pltpu.VMEM)
    dma = pltpu.SemaphoreType.DMA
    out = pl.pallas_call(
        functools.partial(relay_kernel, sections, ticks, cols, requests),
        out_shape=jax.ShapeDtypeStruct((ticks, blocks, HD), bf16),
        in_specs=[pl.BlockSpec(memory_space=pltpu.SMEM), vmem, vmem, vmem,
                  pl.BlockSpec(memory_space=pl.ANY), vmem, vmem, vmem, vmem],
        out_specs=vmem,
        scratch_shapes=[
            pltpu.VMEM(kv_weight.shape[1:], bf16),
            pltpu.VMEM((ticks, requests, QH, HD), bf16),
            pltpu.VMEM((ticks - 1, QH * requests, HD), bf16),
            pltpu.VMEM((QH, requests, HD), f32),
            pltpu.VMEM((KVH, ticks, 2 * GROUP, HD), bf16),
            pltpu.VMEM((requests, ticks, 2 * GROUP, HD), bf16),
            pltpu.VMEM((ticks * 8, HD), f32),
            pltpu.VMEM((requests, ticks * 8, HD), f32),
            pltpu.VMEM((ticks, requests, 3 * HD), f32),
            pltpu.VMEM((ticks, requests, 3 * HD), f32),
            pltpu.VMEM((2 * GROUP, requests, HD), f32),
            pltpu.VMEM((GROUP, requests, HD), f32),
            pltpu.VMEM((ticks - 1, requests * GROUP, HD), bf16),
            pltpu.VMEM((ticks, requests, GROUP, HD), bf16),
            dma((cols,)), dma((120,)), dma((ticks,)), dma((ticks - 1,)),
            dma((2,)), dma((2,)), dma((2,)), dma((ticks,)), dma((ticks,)),
        ],
        compiler_params=pltpu.CompilerParams(
            collective_id=0, has_side_effects=True, vmem_limit_bytes=40 * 1024 * 1024),
        name="relay",
    )(
        lens,
        arriving.reshape(blocks, HD),
        entering.reshape(ticks - 1, blocks, HD),
        gain.reshape(blocks, HD),
        kv_weight[0],
        queries.reshape(ticks, QH, HD),
        cache_keys.reshape(ticks, *cache_keys.shape[3:]),
        cache_values.reshape(ticks, *cache_values.shape[3:]),
        turn,
    )
    return out.reshape(1, ticks, 1, blocks * HD)


def solution(mesh):
    placed = (
        P("section", ("row", "col"), None),
        P(None, ("row", "col"), None),
        P("section", None),
        P("section", "row", "col"),
        P("section", None, ("row", "col"), None),
        P("section", None, ("row", "col"), None, None),
        P("section", None, ("row", "col"), None, None),
        P(None, ("row", "col")),
    )
    fits = mesh.shape["col"] == KVH and mesh.shape["row"] == 2

    def run(*args):
        one_each = args[0].shape[1] == mesh.shape["row"] * mesh.shape["col"]
        body = per_device if fits and one_each else per_device_general
        return jax.shard_map(
            body,
            mesh=mesh,
            in_specs=placed,
            out_specs=P("section", None, ("row", "col"), None),
            check_vma=False,
        )(*args)

    return run
```

```python
import functools

import jax
import jax.numpy as jnp
import numpy as np
from jax import lax
from jax.experimental import pallas as pl
from jax.experimental.pallas import tpu as pltpu
from jax.sharding import PartitionSpec as P

QH = 64
KVH = 4
HD = 128
GROUP = QH // KVH
MESH = pl.DeviceIdType.MESH


def shifted(array, axis, by):
    devices = lax.axis_size(axis)
    pairs = [(i, i + by) for i in range(devices) if 0 <= i + by < devices]
    return lax.ppermute(array, axis, pairs)


def rotate(keys, positions):
    half = HD // 2
    steps_up = jnp.arange(half).astype(jnp.float32)
    inverse = jnp.exp(-jnp.log(jnp.float32(500000.0)) * steps_up / half)
    angle = positions.astype(jnp.float32)[:, None] * inverse[None, :]
    cosine = jnp.cos(angle)[:, None, :]
    sine = jnp.sin(angle)[:, None, :]
    first = keys[..., :half]
    second = keys[..., half:]
    return jnp.concatenate(
        [first * cosine - second * sine, second * cosine + first * sine], axis=-1
    )


def attend(query_row, keys, values, new_key, new_value, length):
    slots = keys.shape[0]
    factor = 1.0 / np.sqrt(HD)
    grouped = query_row.reshape(KVH, QH // KVH, HD)
    cached = keys.reshape(slots, KVH, HD)
    stored = values.reshape(slots, KVH, HD)
    scores = (
        jnp.einsum("ghd,lgd->ghl", grouped, cached, preferred_element_type=jnp.float32) * factor
    )
    live = jnp.arange(slots) < length
    scores = jnp.where(live[None, None, :], scores, jnp.float32(-1e30))
    own = jnp.einsum("ghd,gd->gh", grouped, new_key, preferred_element_type=jnp.float32) * factor
    top = jnp.maximum(jnp.max(scores, axis=-1), own)
    weights = jnp.exp(scores - top[..., None])
    own_weight = jnp.exp(own - top)
    total = jnp.sum(weights, axis=-1) + own_weight
    probs = (weights / total[..., None]).astype(jnp.bfloat16)
    own_prob = (own_weight / total).astype(jnp.bfloat16)
    mixed = jnp.einsum("ghl,lgd->ghd", probs, stored, preferred_element_type=jnp.float32)
    mixed = (
        mixed + own_prob.astype(jnp.float32)[..., None] * new_value.astype(jnp.float32)[:, None, :]
    )
    return mixed.reshape(1, QH * HD)


def per_device_general(arriving, entering, gain, kv_weight, queries, cache_keys, cache_values, lengths):
    section_at = lax.axis_index("section")
    row_at = lax.axis_index("row")
    rows_count = lax.axis_size("row")
    cols_count = lax.axis_size("col")
    ticks = queries.shape[1]
    layers_all = lengths.shape[0] - ticks + 1
    width = arriving.shape[2]
    half_width = width // rows_count
    heads_width = QH * HD
    weight = kv_weight[0]
    gain_row = gain[0].astype(jnp.float32)
    current = arriving[0]
    outputs = []
    for tick in range(ticks):
        if tick > 0:
            passed = shifted(current, "section", 1)
            current = jnp.where(section_at == 0, entering[tick - 1], passed)
        length = lax.dynamic_index_in_dim(
            lengths[:, 0], tick - section_at + layers_all - 1, 0, keepdims=False
        )
        wide = current.astype(jnp.float32)
        scale = lax.rsqrt(jnp.mean(wide * wide, axis=1, keepdims=True) + 1e-05)
        normed = (wide * scale * gain_row[None, :]).astype(jnp.bfloat16)
        mine = lax.dynamic_slice_in_dim(
            lax.all_gather(normed, ("row", "col"), axis=0, tiled=True),
            row_at * half_width,
            half_width,
            1,
        )
        gathered = jnp.dot(mine, weight, preferred_element_type=jnp.float32)
        partial_rows = jnp.swapaxes(gathered.reshape(rows_count, cols_count, -1), 0, 1)
        summed = lax.psum_scatter(partial_rows, "row", scatter_dimension=1, tiled=True)
        fresh = lax.all_to_all(summed, "col", split_axis=0, concat_axis=2, tiled=True)
        fresh = fresh.reshape(KVH, 2, HD)
        new_key = rotate(fresh[None, :, 0, :], length[None])[0].astype(jnp.bfloat16)
        new_value = fresh[:, 1, :].astype(jnp.bfloat16)
        mixed = attend(
            queries[0, tick, 0],
            cache_keys[0, tick, 0],
            cache_values[0, tick, 0],
            new_key,
            new_value,
            length,
        )
        joined = jnp.concatenate([wide[:, :heads_width] + mixed, wide[:, heads_width:]], axis=1)
        current = joined.astype(jnp.bfloat16)
        outputs.append(current)
    return jnp.stack(outputs, axis=0)[None]


def relay_kernel(
    sections, ticks, cols, requests,
    lens_ref, arr_ref, ent_ref, gain_ref, w_ref, q_ref, k_ref, v_ref,
    out_ref,
    wv, kv, vv, rows_bf, gain_f, xj, xh, qb_src, qb_buf, misc_src, misc_buf, p_src, p_buf,
    hj, lse_hj, xo, oj,
    w_sem, k_sem, v_sem, send_sem, xj_sem, xh_sem, qb_sem, misc_sem, p_sem, z_sem, out_sem,
):
    f32, bf16 = jnp.float32, jnp.bfloat16
    me_s, me_r, me_c = lax.axis_index("section"), lax.axis_index("row"), lax.axis_index("col")
    me_j = me_r * cols + me_c
    factor = 1.0 / np.sqrt(HD)
    width = 2.0 * QH * HD
    later = ticks - 1

    def at(s, r, c):
        return {"section": s, "row": r, "col": c}

    barrier = pltpu.get_barrier_semaphore()

    def greet(cond, where):
        def do():
            pl.semaphore_signal(barrier, inc=1, device_id=where, device_id_type=MESH)
        if cond is True:
            do()
        else:
            pl.when(cond)(do)

    for dr in range(2):
        for dc in range(cols):
            if dr or dc:
                greet(True, at(me_s, (me_r + dr) % 2, (me_c + dc) % cols))
    for d in range(1, ticks):
        greet(me_s >= d, at(me_s - d, me_r, me_c))
    for dc in range(1, cols):
        greet((me_r == 0) & (me_s >= 1), at(me_s - 1, me_r, (me_c + dc) % cols))

    depth = w_ref.shape[0] // cols

    def cache_copy(t):
        return (pltpu.make_async_copy(k_ref.at[t], kv.at[t], k_sem.at[t]),
                pltpu.make_async_copy(v_ref.at[t], vv.at[t], v_sem.at[t]))

    def w_copy(b):
        span = pl.ds(b * depth, depth)
        return pltpu.make_async_copy(w_ref.at[span], wv.at[span], w_sem.at[b])

    for copy in cache_copy(0):
        copy.start()
    for b in range(cols):
        w_copy(b).start()
    for t in range(1, ticks):
        for copy in cache_copy(t):
            copy.start()

    def blocked(x):
        count = x.shape[1] // HD
        return jnp.swapaxes(jnp.stack([x[:, h * HD:(h + 1) * HD] for h in range(count)]), 0, 1)

    held_rows = jnp.concatenate(
        [arr_ref[...].astype(f32), ent_ref[...].astype(f32), gain_ref[...].astype(f32),
         jnp.zeros((7 - ticks, arr_ref.shape[1]), f32)], axis=0)
    held_rows = blocked(held_rows)
    rows_bf[...] = held_rows[:ticks].astype(bf16)
    gain_f[...] = held_rows[ticks]

    out_ref[0, QH:] = rows_bf[0, QH:]
    for t in range(1, ticks):
        @pl.when(me_s < t)
        def _():
            out_ref[t, QH:] = rows_bf[t - me_s, QH:]

    reach = jnp.minimum(ticks - 1, sections - 1 - me_s)
    onward = jnp.where((me_r == 0) & (me_s + 1 < sections), cols - 1, 0)
    pl.semaphore_wait(barrier, 2 * cols - 1 + reach + onward)

    sent = []
    on_chain, off_chain, has_next = me_r == 0, me_r == 1, me_s + 1 < sections
    chain_next = on_chain & has_next

    def remote(cond, src, dst, rsem, where, held=None, like=None):
        number = len(sent)
        sent.append((cond if held is None else held, (lambda: src) if like is None else like))

        def go():
            pltpu.make_async_remote_copy(
                src_ref=src, dst_ref=dst, send_sem=send_sem.at[number], recv_sem=rsem,
                device_id=where, device_id_type=MESH).start()
        if cond is True:
            go()
        else:
            pl.when(cond)(go)

    def local(cond, src, dst, rsem):
        def go():
            pltpu.make_async_copy(src, dst, rsem).start()
        pl.when(cond)(go)

    def push(cond, src_of, dst, rsem, row):
        for dc in range(cols):
            col = (me_c + dc) % cols
            if dc == 0:
                here = me_r == row if cond is True else cond & (me_r == row)
                away = me_r != row if cond is True else cond & (me_r != row)
                local(here, src_of(col), dst, rsem)
                remote(away, src_of(col), dst, rsem, at(me_s, row, col))
            else:
                remote(cond, src_of(col), dst, rsem, at(me_s, row, col))

    def landed(ref, sem):
        pltpu.make_async_copy(ref, ref, sem).wait()

    def length_of(t):
        return lens_ref[0, t - me_s + sections - 1]

    def cache_part(t):
        length = length_of(t)
        for copy in cache_copy(t):
            copy.wait()
        lane = lax.broadcasted_iota(jnp.int32, (GROUP, HD), 1)
        sub = lax.broadcasted_iota(jnp.int32, (GROUP, HD), 0)
        lse_row = jnp.zeros((1, HD), f32)
        for g in range(KVH):
            qg = q_rows[t, g * GROUP:(g + 1) * GROUP, :].astype(bf16)
            kg = kv[t, :, g * HD:(g + 1) * HD]
            vg = vv[t, :, g * HD:(g + 1) * HD]
            s = lax.dot_general(qg, kg, (((1,), (1,)), ((), ())), preferred_element_type=f32) * factor
            s = jnp.where(lane < length, s, f32(-1e30))
            top = jnp.max(s, axis=1, keepdims=True)
            e = jnp.exp(s - top)
            total = jnp.sum(e, axis=1, keepdims=True)
            base = jnp.dot((e / total).astype(bf16), vg, preferred_element_type=f32)
            qb_src[g, t, :GROUP, :] = qg
            qb_src[g, t, GROUP:, :] = base.astype(bf16)
            lse = top + jnp.log(total)
            lse_row += jnp.sum(jnp.where(lane == sub + g * GROUP, lse, 0.0), axis=0, keepdims=True)
        misc_src[t * 8:t * 8 + 8, :] = jnp.concatenate(
            [cosines[t:t + 1], sines[t:t + 1], lse_row, jnp.zeros((5, HD), f32)], axis=0)

    def push_cache_part(first, count, number):
        span = pl.ds(first, count)
        push(True, lambda col: qb_src.at[col, span], qb_buf.at[me_j, span], qb_sem.at[number], 0)
        push(True, lambda col: misc_src.at[pl.ds(first * 8, count * 8)],
             misc_buf.at[me_j, pl.ds(first * 8, count * 8)], misc_sem.at[number], 0)

    push(True, lambda col: rows_bf.at[0, pl.ds(QH, QH)], xj.at[0, me_j], xj_sem.at[0], 1)
    push(True, lambda col: rows_bf.at[0, pl.ds(0, QH)], xj.at[0, me_j], xj_sem.at[0], 0)
    for d in range(1, ticks):
        remote(me_s + d < sections, rows_bf.at[0, pl.ds(QH, QH)], out_ref.at[d, pl.ds(QH, QH)],
               z_sem.at[d], at(me_s + d, me_r, me_c))

    half = HD // 2
    tick_of = lax.broadcasted_iota(jnp.int32, (8, HD), 0)
    lane_of = lax.broadcasted_iota(jnp.int32, (8, HD), 1)
    step = jnp.where(lane_of < half, lane_of, lane_of - half).astype(f32)
    place = jnp.zeros((8, HD), f32)
    for t in range(ticks):
        place = jnp.where(tick_of == t, length_of(t).astype(f32), place)
    angle = place * jnp.exp(-jnp.log(f32(500000.0)) * step / half)
    cosines = jnp.cos(angle)
    sines = jnp.where(lane_of < half, -jnp.sin(angle), jnp.sin(angle))
    q_rows = blocked(q_ref[...].astype(f32))

    cache_part(0)
    push_cache_part(0, 1, 0)

    for t in range(1, ticks):
        push(me_s == 0, lambda col: rows_bf.at[t, pl.ds(0, QH)], xj.at[t, me_j], xj_sem.at[t], 0)
    for t in range(1, ticks):
        @pl.when(me_s >= t)
        def _():
            landed(out_ref.at[t, pl.ds(QH, QH)], z_sem.at[t])
        push(True, lambda col: out_ref.at[t, pl.ds(QH, QH)], xj.at[t, me_j], xj_sem.at[t], 1)

    def rest():
        for t in range(1, ticks):
            cache_part(t)
        push_cache_part(1, later, 1)

    def turned(t):
        return jnp.swapaxes(xj[t].astype(f32), 0, 1)

    def lanes(x, gains):
        return jnp.concatenate([x[h] * gains[h:h + 1] for h in range(GROUP)], axis=1)

    def squares(x):
        return jnp.sum(jnp.sum(x * x, axis=0), axis=1, keepdims=True)

    def static_part(first, count):
        gains = gain_f[QH:]
        for t in range(first, first + count):
            landed(xj.at[t], xj_sem.at[t])
        xt = [turned(t) for t in range(first, first + count)]
        total = jnp.zeros((count * requests, 2 * HD), f32)
        for b in range(cols):
            heads = slice(b * GROUP, (b + 1) * GROUP)
            lhs = jnp.concatenate([lanes(x[heads], gains[heads]) for x in xt], axis=0).astype(bf16)
            total += jnp.dot(lhs, wv[b * depth:(b + 1) * depth, :], preferred_element_type=f32)
        for i in range(count):
            p_src[first + i, :, :2 * HD] = total[i * requests:(i + 1) * requests]
            p_src[first + i, :, 2 * HD:] = jnp.broadcast_to(squares(xt[i]), (requests, HD))

    rows = requests * GROUP

    def prepare(t):
        def lay():
            landed(xj.at[t], xj_sem.at[t])
            xh[t] = turned(t).reshape(QH * requests, HD).astype(bf16)
        if t == 0:
            lay()
        else:
            pl.when(me_s == 0)(lay)
        if t <= 1:
            number, first, count = (0, 0, 1) if t == 0 else (1, 1, later)
            landed(qb_buf.at[:, pl.ds(first, count)], qb_sem.at[number])
            landed(misc_buf.at[:, pl.ds(first * 8, count * 8)], misc_sem.at[number])
        hj[...] = jnp.swapaxes(qb_buf[:, t].astype(f32), 0, 1)
        sums = jnp.concatenate([misc_buf[j, t * 8 + 2:t * 8 + 3, :] for j in range(requests)], axis=0)
        lane = lax.broadcasted_iota(jnp.int32, (GROUP, requests, HD), 2)
        head = lax.broadcasted_iota(jnp.int32, (GROUP, requests, HD), 0) + me_c * GROUP
        picked = jnp.sum(jnp.where(lane == head, sums[None], 0.0), axis=2, keepdims=True)
        lse_hj[...] = jnp.broadcast_to(picked, (GROUP, requests, HD))

    def chain(t):
        fresh = jnp.zeros((requests, 2 * HD), f32)
        power = jnp.zeros((requests, 1), f32)
        own_rows = None
        for k in range(cols):
            b = (me_c + cols - k) % cols
            span = pl.ds(pl.multiple_of(b * rows, rows), rows)
            if t > 0:
                @pl.when(me_s > 0)
                def _():
                    landed(xh.at[t, pl.ds(0, rows)], xh_sem.at[t - 1, k])
            x = xh[t, span, :].astype(f32).reshape(GROUP, requests, HD)
            own_rows = x if k == 0 else own_rows
            gains = gain_f[pl.ds(pl.multiple_of(b * GROUP, GROUP), GROUP), :]
            fresh += jnp.dot(lanes(x, gains).astype(bf16),
                             wv[pl.ds(pl.multiple_of(b * depth, depth), depth), :],
                             preferred_element_type=f32)
            power += squares(x)
        if t <= 1:
            span = pl.ds(0, 1) if t == 0 else pl.ds(1, later)
            landed(p_buf.at[span], p_sem.at[t])
        power += p_buf[t, :, 2 * HD:2 * HD + 1]
        fresh = (fresh + p_buf[t, :, :2 * HD]) * lax.rsqrt(power / width + 1e-05)
        cosine = jnp.concatenate([misc_buf[j, t * 8:t * 8 + 1, :] for j in range(requests)], axis=0)
        sine = jnp.concatenate([misc_buf[j, t * 8 + 1:t * 8 + 2, :] for j in range(requests)], axis=0)
        key = fresh[:, :HD]
        key = key * cosine + pltpu.roll(key, HD // 2, 1) * sine
        key = key.astype(bf16).astype(f32)
        value = fresh[:, HD:].astype(bf16).astype(f32)
        q = hj[:GROUP]
        base = hj[GROUP:]
        lse = lse_hj[...]
        own = jnp.sum(q * key[None], axis=2, keepdims=True) * factor
        top = jnp.maximum(lse, own)
        old_weight = jnp.exp(lse - top)
        own_weight = jnp.exp(own - top)
        inverse = 1.0 / (old_weight + own_weight)
        own_prob = (own_weight * inverse).astype(bf16).astype(f32)
        mixed = base * (old_weight * inverse) + own_prob * value[None]
        mine = own_rows + mixed
        block = pl.ds(pl.multiple_of(me_c * GROUP, GROUP), GROUP)
        if t + 1 < ticks:
            xo[t] = mine.reshape(rows, HD).astype(bf16)
            for dc in range(cols):
                remote(has_next, xo.at[t],
                       xh.at[t + 1, pl.ds(pl.multiple_of(me_c * rows, rows), rows)],
                       xh_sem.at[t, dc], at(me_s + 1, 0, (me_c + dc) % cols), held=chain_next, like=lambda: xo.at[t])
        oj[t] = jnp.swapaxes(mine, 0, 1).astype(bf16)
        for r in range(2):
            for dc in range(cols):
                col = (me_c + dc) % cols
                src = oj.at[t, r * cols + col]
                dst = out_ref.at[t, block]
                if r == 0 and dc == 0:
                    pltpu.make_async_copy(src, dst, out_sem.at[t]).start()
                else:
                    remote(True, src, dst, out_sem.at[t], at(me_s, r, col),
                           held=on_chain, like=lambda: oj.at[t, 0])

    def push_static(first, count):
        span = pl.ds(first, count)
        remote(True, p_src.at[span], p_buf.at[span], p_sem.at[0 if first == 0 else 1],
               at(me_s, 0, me_c), held=off_chain, like=lambda: p_src.at[span])

    for b in range(cols):
        w_copy(b).wait()

    @pl.when(me_r == 0)
    def _():
        prepare(0)
        chain(0)

    @pl.when(me_r == 1)
    def _():
        static_part(0, 1)
        push_static(0, 1)

    rest()

    @pl.when(me_r == 1)
    def _():
        static_part(1, later)
        push_static(1, later)

    @pl.when(me_r == 0)
    def _():
        for t in range(1, ticks):
            prepare(t)
            chain(t)

    for t in range(ticks):
        landed(out_ref.at[t, pl.ds(0, QH)], out_sem.at[t])
    for number, (cond, like) in enumerate(sent):
        def done(number=number, like=like):
            landed(like(), send_sem.at[number])
        if cond is True:
            done()
        else:
            pl.when(cond)(done)


def per_device(arriving, entering, gain, kv_weight, queries, cache_keys, cache_values, lengths):
    sections, cols = lax.axis_size("section"), lax.axis_size("col")
    ticks = queries.shape[1]
    requests = 2 * cols
    blocks = arriving.shape[2] // HD
    bf16, f32 = jnp.bfloat16, jnp.float32
    vmem = pl.BlockSpec(memory_space=pltpu.VMEM)
    hbm = pl.BlockSpec(memory_space=pltpu.HBM)
    dma = pltpu.SemaphoreType.DMA
    out = pl.pallas_call(
        functools.partial(relay_kernel, sections, ticks, cols, requests),
        out_shape=jax.ShapeDtypeStruct((ticks, blocks, HD), bf16),
        in_specs=[pl.BlockSpec(memory_space=pltpu.SMEM), vmem, vmem, vmem, hbm, vmem, hbm, hbm],
        out_specs=vmem,
        scratch_shapes=[
            pltpu.VMEM(kv_weight.shape[1:], bf16),
            pltpu.VMEM((ticks, *cache_keys.shape[3:]), bf16),
            pltpu.VMEM((ticks, *cache_values.shape[3:]), bf16),
            pltpu.VMEM((ticks, blocks, HD), bf16),
            pltpu.VMEM((blocks, HD), f32),
            pltpu.VMEM((ticks, requests, QH, HD), bf16),
            pltpu.VMEM((ticks, QH * requests, HD), bf16),
            pltpu.VMEM((KVH, ticks, 2 * GROUP, HD), bf16),
            pltpu.VMEM((requests, ticks, 2 * GROUP, HD), bf16),
            pltpu.VMEM((ticks * 8, HD), f32),
            pltpu.VMEM((requests, ticks * 8, HD), f32),
            pltpu.VMEM((ticks, requests, 3 * HD), f32),
            pltpu.VMEM((ticks, requests, 3 * HD), f32),
            pltpu.VMEM((2 * GROUP, requests, HD), f32),
            pltpu.VMEM((GROUP, requests, HD), f32),
            pltpu.VMEM((ticks - 1, requests * GROUP, HD), bf16),
            pltpu.VMEM((ticks, requests, GROUP, HD), bf16),
            dma((cols,)), dma((ticks,)), dma((ticks,)), dma((120,)), dma((ticks,)),
            dma((ticks - 1, cols)),
            dma((2,)), dma((2,)), dma((2,)), dma((ticks,)), dma((ticks,)),
        ],
        compiler_params=pltpu.CompilerParams(
            collective_id=0, has_side_effects=True, vmem_limit_bytes=60 * 1024 * 1024),
        name="relay",
    )(
        lengths.reshape(1, -1),
        arriving.reshape(1, -1),
        entering.reshape(ticks - 1, -1),
        gain,
        kv_weight[0],
        queries.reshape(ticks, -1),
        cache_keys.reshape(ticks, *cache_keys.shape[3:]),
        cache_values.reshape(ticks, *cache_values.shape[3:]),
    )
    return out.reshape(1, ticks, 1, blocks * HD)


def solution(mesh):
    placed = (
        P("section", ("row", "col"), None),
        P(None, ("row", "col"), None),
        P("section", None),
        P("section", "row", "col"),
        P("section", None, ("row", "col"), None),
        P("section", None, ("row", "col"), None, None),
        P("section", None, ("row", "col"), None, None),
        P(None, ("row", "col")),
    )
    fits = mesh.shape["col"] == KVH and mesh.shape["row"] == 2

    def run(*args):
        one_each = args[0].shape[1] == mesh.shape["row"] * mesh.shape["col"]
        body = per_device if fits and one_each else per_device_general
        return jax.shard_map(
            body,
            mesh=mesh,
            in_specs=placed,
            out_specs=P("section", None, ("row", "col"), None),
            check_vma=False,
        )(*args)

    return run
```
